32 devices in a mesh: gx: 2 (over y), gy: 4 (over x, core), gz: 4 (over z).
Axes of the slice: x: 2, y: 2, z: 4, core: 2. Of those that a mesh axis runs over, the one named last changes fastest.
Arguments:
- right_side: float32 [16, 128, 1024], P('gx', 'gy', 'gz'), may hold values from -60 to 60
- wavenumber_sq: float32 [16, 128, 1024], P('gx', 'gy', 'gz'), may hold values from 0.3 to 1.5
- sketch_matrix: float32 [16, 16, 128, 1024], P(None, 'gx', 'gy', 'gz'), may hold values from -1.5 to 1.5
Outputs:
- solution: float32 [16, 128, 1024], P('gx', 'gy', 'gz')
- residual: float32 [16, 128, 1024], P('gx', 'gy', 'gz')
The draws below stay inside these ranges and needn't reach their ends.
All inputs are finite; a program needn't handle non-finite values.
Results may differ from the reference program's by a relative error of at most 0.0003.
Values sent between devices are 32-bit elements; how exact they have to be, the bound alone decides.
A program may use at most 64 MiB of HBM per device.

```python
import math
import jax
import jax.numpy as jnp
from jax import lax

SK = 16
SWEEPS = 3
ITERS = 3
NX = 16
NY = 128
NZ = 1024


def draw_right_side(key, part):
    first_key = jax.random.fold_in(key, 11)
    xcoord = jnp.arange(NX, dtype=jnp.float32) / NX
    ycoord = jnp.arange(NY, dtype=jnp.float32) / NY
    zcoord = jnp.arange(NZ, dtype=jnp.float32) / NZ
    ramp = (xcoord[:, None, None] + ycoord[None, :, None] + zcoord[None, None, :]) / 3.0
    growth = jnp.exp(math.log(3.0) * ramp)
    noise = jnp.clip(jax.random.normal(first_key, (NX, NY, NZ), jnp.float32), -6.0, 6.0)
    values = noise * growth
    return values.astype(jnp.float32)


def block_scale(key, extent, split, low, top_value):
    level = 1.0
    for axis_at, blocks in split:
        steps = jax.random.uniform(jax.random.fold_in(jax.random.fold_in(key, 6), axis_at), (blocks,), jnp.float32, low / len(split), top_value / len(split))
        level = level * jnp.repeat(jnp.exp(steps), extent[axis_at] // blocks).reshape((-1,) + (1,) * (len(extent) - 1 - axis_at))
    return level


def bell_draw(stream_key, extent, deviation, reach, split=(), kind=jnp.bfloat16):
    array = jax.random.normal(stream_key, extent, jnp.float32) * deviation
    if len(split) > 0:
        array = block_scale(stream_key, extent, split, -0.22, 0.18) * array
    return jnp.clip(array, min=-reach, max=reach).astype(kind)


def setup_inputs(seed: int = 0) -> dict:
    streams_of = jax.random.split(jax.random.key(seed), 4)
    right_side = draw_right_side(jax.random.fold_in(streams_of[3], 71), 0)
    wavenumber_sq = jnp.clip(jnp.exp(math.log(1.5) - 1.60943787 * jax.random.uniform(streams_of[1], (NX, NY, NZ), jnp.float32) ** block_scale(streams_of[1], (NX, NY, NZ), ((0, 2), (1, 4), (2, 4)), -0.2, 0.2)), 0.3, 1.5)
    sketch_matrix = bell_draw(streams_of[2], (SK, NX, NY, NZ), SK ** -0.5, 1.5, ((1, 2), (2, 4), (3, 4)), jnp.float32)
    return {"right_side": right_side, "wavenumber_sq": wavenumber_sq, "sketch_matrix": sketch_matrix}


HIGH = lax.Precision.HIGHEST

def neighbours(grid_field):
    total = jnp.roll(grid_field, 1, 0) + jnp.roll(grid_field, -1, 0)
    total = total + jnp.roll(grid_field, 1, 1) + jnp.roll(grid_field, -1, 1)
    total = total + jnp.roll(grid_field, 1, 2) + jnp.roll(grid_field, -1, 2)
    return total

def smoother(vector, wavenumber_sq):
    diagonal = 6.0 + wavenumber_sq
    result = vector / diagonal
    for sweep_idx in range(SWEEPS):
        result = result + (vector - (diagonal * result - neighbours(result))) / diagonal
    return result

def helmholtz(grid_field, wavenumber_sq):
    return (6.0 - wavenumber_sq) * grid_field - neighbours(grid_field)

def sketched(sketch_rows, grid_field):
    return jnp.dot(sketch_rows, grid_field.reshape(-1), precision=HIGH, preferred_element_type=jnp.float32)

def solve_small(hessen, beta_norm):
    target = jnp.zeros((ITERS + 1,), jnp.float32).at[0].set(beta_norm)
    basis = []
    upper = [[None] * ITERS for row_idx in range(ITERS)]
    for col_idx in range(ITERS):
        column = hessen[:, col_idx]
        for row_idx in range(col_idx):
            factor = jnp.sum(basis[row_idx] * column)
            upper[row_idx][col_idx] = factor
            column = column - factor * basis[row_idx]
        diag_term = jnp.sqrt(jnp.sum(column * column))
        upper[col_idx][col_idx] = diag_term
        basis.append(column / diag_term)
    projected = [jnp.sum(member * target) for member in basis]
    coeffs = [None] * ITERS
    for row_idx in reversed(range(ITERS)):
        accum = projected[row_idx]
        for col_idx in range(row_idx + 1, ITERS):
            accum = accum - upper[row_idx][col_idx] * coeffs[col_idx]
        coeffs[row_idx] = accum / upper[row_idx][row_idx]
    weights = jnp.stack(coeffs)
    leftover = target - jnp.dot(hessen, weights, precision=HIGH)
    return (weights, leftover)

def reference(right_side, wavenumber_sq, sketch_matrix):
    sketch_rows = sketch_matrix.reshape(SK, -1)
    rhs_sketch = sketched(sketch_rows, right_side)
    beta_norm = jnp.sqrt(jnp.sum(rhs_sketch * rhs_sketch))
    vectors = [right_side / beta_norm]
    images = [rhs_sketch / beta_norm]
    directions = []
    hessen = jnp.zeros((ITERS + 1, ITERS), jnp.float32)
    for iteration in range(ITERS):
        direction = smoother(vectors[-1], wavenumber_sq)
        directions.append(direction)
        product = helmholtz(direction, wavenumber_sq)
        sketch_new = sketched(sketch_rows, product)
        stacked = jnp.stack(images, axis=1)
        weights = jnp.dot(sketch_new, stacked, precision=HIGH)
        remainder = product
        for member in range(iteration + 1):
            remainder = remainder - weights[member] * vectors[member]
        sketch_rem = sketched(sketch_rows, remainder)
        length = jnp.sqrt(jnp.sum(sketch_rem * sketch_rem))
        vectors.append(remainder / length)
        images.append(sketch_rem / length)
        hessen = hessen.at[:iteration + 1, iteration].set(weights)
        hessen = hessen.at[iteration + 1, iteration].set(length)
    coeffs, leftover = solve_small(hessen, beta_norm)
    solution = directions[0] * coeffs[0]
    for member in range(1, ITERS):
        solution = solution + directions[member] * coeffs[member]
    residual = vectors[0] * leftover[0]
    for member in range(1, ITERS + 1):
        residual = residual + vectors[member] * leftover[member]
    return (solution, residual)
```

```python
import functools

import jax
import jax.numpy as jnp
from jax import lax
from jax.experimental import pallas as pl
from jax.experimental.pallas import tpu as pltpu
from jax.sharding import PartitionSpec as P

SWEEPS = 3
ITERS = 3
DEPTH = SWEEPS + 1
SHIFTS = (0.75, 0.5, 0.25)
MESH = pl.DeviceIdType.MESH
LANES = 128


def small_solve(sketches):
    def dot(a, b):
        return jnp.sum(a * b, axis=0, keepdims=True)

    beta = jnp.sqrt(dot(sketches[0], sketches[0]))
    combos = [[1.0 / beta]]
    images = [sketches[0] / beta]
    hessen = []
    for it in range(ITERS):
        a = combos[it]
        b = [SHIFTS[i] * a[i] for i in range(it + 1)] + [None]
        for i in range(1, it + 2):
            b[i] = a[i - 1] if b[i] is None else b[i] + a[i - 1]
        s = b[0] * sketches[0]
        for i in range(1, it + 2):
            s = s + b[i] * sketches[i]
        c = [dot(images[i], s) for i in range(it + 1)]
        t = s
        for i in range(it + 1):
            t = t - c[i] * images[i]
            for m in range(i + 1):
                b[m] = b[m] - c[i] * combos[i][m]
        nu = jnp.sqrt(dot(t, t))
        images.append(t / nu)
        combos.append([x / nu for x in b])
        hessen.append(c + [nu])

    def vdot(a, b):
        total = a[0] * b[0]
        for i in range(1, min(len(a), len(b))):
            total = total + a[i] * b[i]
        return total

    basis, upper = [], [[None] * ITERS for _ in range(ITERS)]
    for col in range(ITERS):
        column = list(hessen[col])
        for row in range(col):
            factor = vdot(basis[row], column)
            upper[row][col] = factor
            for i in range(len(basis[row])):
                column[i] = column[i] - factor * basis[row][i]
        norm = jnp.sqrt(vdot(column, column))
        upper[col][col] = norm
        basis.append([x / norm for x in column])
    y = [None] * ITERS
    for row in reversed(range(ITERS)):
        acc = basis[row][0] * beta
        for col in range(row + 1, ITERS):
            acc = acc - upper[row][col] * y[col]
        y[row] = acc / upper[row][row]
    e = []
    for i in range(ITERS + 1):
        acc = beta if i == 0 else jnp.zeros_like(beta)
        for col in range(ITERS):
            if i <= col + 1:
                acc = acc - hessen[col][i] * y[col]
        e.append(acc)
    sol, res = [], []
    for i in range(ITERS):
        acc = y[i] * combos[i][i]
        for j in range(i + 1, ITERS):
            acc = acc + y[j] * combos[j][i]
        sol.append(acc)
    for i in range(ITERS + 1):
        acc = e[i] * combos[i][i]
        for j in range(i + 1, ITERS + 1):
            acc = acc + e[j] * combos[j][i]
        res.append(acc)
    return sol, res


def kernel(sizes, r_ref, k_ref, s_ref, sol_ref, res_ref,
           sk, ksq, dinv, basis, last, za, zb, pk,
           ysend, yrecv, zsend, zrecv, crecv, red0, red1, red2, got1, got2,
           local_sem, gsend, grecv, xsend, xrecv, rsend1, rrecv1, rsend2, rrecv2):
    nx, ny, nz = sizes
    bx, by, bz = r_ref.shape
    rows = sk.shape[0]
    X, Y, Z = nx * bx, by + 2 * DEPTH, bz + LANES
    half = X // 2
    per = LANES // DEPTH
    groups = zsend.shape[-1] // LANES
    gx, gy, gz = lax.axis_index("gx"), lax.axis_index("gy"), lax.axis_index("gz")

    def wrap(i, n):
        return lax.rem(i + n, n)

    py, qy = wrap(gy - 1, ny), wrap(gy + 1, ny)
    pz, qz = wrap(gz - 1, nz), wrap(gz + 1, nz)

    plane_peers = []
    for dx in range(nx):
        for dy in range(ny):
            if dx or dy:
                plane_peers.append((wrap(gx + dx, nx), wrap(gy + dy, ny), gz))
    z_peers = [(gx, gy, wrap(gz + d, nz)) for d in range(1, nz)]
    diagonals = [(gx, py, pz), (gx, qy, pz), (gx, py, qz), (gx, qy, qz)]

    own_s = pltpu.make_async_copy(s_ref, sk, local_sem.at[0])
    own_k = pltpu.make_async_copy(
        k_ref, ksq.at[pl.ds(0, bx), pl.ds(0, by), pl.ds(0, bz)], local_sem.at[1])
    own_r = pltpu.make_async_copy(
        r_ref, basis.at[0, pl.ds(0, bx), pl.ds(0, by), pl.ds(0, bz)], local_sem.at[2])
    own_k.start()
    own_r.start()
    own_s.start()

    barrier = pltpu.get_barrier_semaphore()
    everyone = plane_peers + z_peers + diagonals
    for peer in everyone:
        pl.semaphore_signal(barrier, inc=1, device_id=peer, device_id_type=MESH)
    pl.semaphore_wait(barrier, len(everyone))

    gathers = []
    for which, src in ((0, k_ref), (1, r_ref)):
        for i in range(1, nx):
            dst = ksq if which == 0 else basis.at[0]
            copy = pltpu.make_async_remote_copy(
                src_ref=src,
                dst_ref=dst.at[pl.ds(i * bx, bx), pl.ds(0, by), pl.ds(0, bz)],
                send_sem=gsend.at[which, i - 1], recv_sem=grecv.at[which, i - 1],
                device_id=(wrap(gx - i, nx), gy, gz), device_id_type=MESH)
            copy.start()
            gathers.append((which, copy))

    sub_low = lax.broadcasted_iota(jnp.int32, (8, bz), 0) < DEPTH
    sub_low_z = lax.broadcasted_iota(jnp.int32, (8, zsend.shape[-1]), 0) < DEPTH
    lane_by = lax.broadcasted_iota(jnp.int32, (by, LANES), 1)
    lane_y = lax.broadcasted_iota(jnp.int32, (Y, LANES), 1)

    pending = []

    def exchange_start(slot, buf):
        def pack_y(p, carry):
            low0, low1 = buf[p, 0:8, 0:bz], buf[p + half, 0:8, 0:bz]
            high0, high1 = buf[p, by - 8:by, 0:bz], buf[p + half, by - 8:by, 0:bz]
            ysend[slot, 0, p] = jnp.where(sub_low, low0, pltpu.roll(low1, DEPTH, 0))
            ysend[slot, 1, p] = jnp.where(sub_low, pltpu.roll(high0, DEPTH, 0), high1)
            return carry

        lax.fori_loop(0, half, pack_y, 0)
        copies = []

        def send(m, src, dst, peer):
            copy = pltpu.make_async_remote_copy(
                src_ref=src, dst_ref=dst, send_sem=xsend.at[slot, m], recv_sem=xrecv.at[slot, m],
                device_id=peer, device_id_type=MESH)
            copy.start()
            copies.append(copy)

        send(0, ysend.at[slot, 0], yrecv.at[slot, 0], (gx, py, gz))
        send(1, ysend.at[slot, 1], yrecv.at[slot, 1], (gx, qy, gz))
        for g in range(groups):
            def pack_z(p, carry):
                left, right = carry
                plane = g * per + p
                mine = lax.div(lane_by, DEPTH) == p
                first = pltpu.roll(buf[plane, 0:by, 0:LANES], DEPTH * p, 1)
                final = pltpu.roll(
                    buf[plane, 0:by, bz - LANES:bz], lax.rem(DEPTH * (p + 1), LANES), 1)
                return jnp.where(mine, first, left), jnp.where(mine, final, right)

            zero = jnp.zeros((by, LANES), jnp.float32)
            left, right = lax.fori_loop(0, min(per, X - g * per), pack_z, (zero, zero))
            zsend[slot, 0, :, g * LANES:(g + 1) * LANES] = left
            zsend[slot, 1, :, g * LANES:(g + 1) * LANES] = right
        send(2, zsend.at[slot, 0], zrecv.at[slot, 0], (gx, gy, pz))
        send(3, zsend.at[slot, 1], zrecv.at[slot, 1], (gx, gy, qz))
        for m, (side, row, peer) in enumerate((
                (0, 0, (gx, py, pz)), (0, by - 8, (gx, qy, pz)),
                (1, 0, (gx, py, qz)), (1, by - 8, (gx, qy, qz)))):
            send(4 + m, zsend.at[slot, side, pl.ds(row, 8)], crecv.at[slot, m], peer)
        pending.extend(copies)
        return copies

    def exchange_finish(slot, buf, copies):
        copies[0].wait_recv()
        copies[1].wait_recv()

        def unpack_y(p, carry):
            up, down = yrecv[slot, 0, p], yrecv[slot, 1, p]
            buf[p, by:Y, 0:bz] = jnp.where(sub_low, up, pltpu.roll(down, DEPTH, 0))
            buf[p + half, by:Y, 0:bz] = jnp.where(sub_low, pltpu.roll(up, DEPTH, 0), down)
            return carry

        lax.fori_loop(0, half, unpack_y, 0)
        for copy in copies[2:]:
            copy.wait_recv()
        right = jnp.concatenate(
            [zrecv[slot, 0], jnp.where(sub_low_z, crecv[slot, 0], crecv[slot, 1])], axis=0)
        left = jnp.concatenate(
            [zrecv[slot, 1], jnp.where(sub_low_z, crecv[slot, 2], crecv[slot, 3])], axis=0)
        for g in range(groups):
            right_g = right[:, g * LANES:(g + 1) * LANES]
            left_g = left[:, g * LANES:(g + 1) * LANES]

            def unpack_z(p, carry):
                high = pltpu.roll(right_g, lax.rem(LANES - DEPTH * p, LANES), 1)
                low = pltpu.roll(left_g, LANES - DEPTH - DEPTH * p, 1)
                tile = jnp.where(
                    lane_y < DEPTH, high, jnp.where(lane_y >= LANES - DEPTH, low, 0.0))
                buf[g * per + p, :, bz:Z] = tile
                return carry

            lax.fori_loop(0, min(per, X - g * per), unpack_z, 0)

    def near(z_ref, p):
        centre = z_ref[p]
        total = z_ref[lax.rem(p + X - 1, X)] + z_ref[lax.rem(p + 1, X)]
        total = total + pltpu.roll(centre, 1, 0) + pltpu.roll(centre, Y - 1, 0)
        total = total + pltpu.roll(centre, 1, 1) + pltpu.roll(centre, Z - 1, 1)
        return centre, total

    def sketch(slot, plane_of):
        def body(p, acc):
            v = plane_of(p)
            out = []
            for row in range(rows):
                prod = sk[row, p] * v
                part = prod[:, 0:LANES]
                for i in range(1, bz // LANES):
                    part = part + prod[:, i * LANES:(i + 1) * LANES]
                tile = part[0:8]
                for i in range(1, by // 8):
                    tile = tile + part[8 * i:8 * i + 8]
                out.append(acc[row] + tile)
            return tuple(out)

        acc = lax.fori_loop(0, bx, body, tuple(jnp.zeros((8, LANES), jnp.float32) for _ in range(rows)))
        for row in range(rows):
            red0[slot, pl.ds(row, 1)] = jnp.sum(acc[row], axis=0, keepdims=True)

    own_k.wait()
    for which, copy in gathers:
        if which == 0:
            copy.wait_recv()
    k_copies = exchange_start(0, ksq)
    own_r.wait()
    own_s.wait()
    sketch(0, lambda p: basis[0, p, 0:by, 0:bz])
    exchange_finish(0, ksq, k_copies)

    def invert(p, carry):
        dinv[p] = 1.0 / (6.0 + ksq[p])
        return carry

    lax.fori_loop(0, X, invert, 0)
    for which, copy in gathers:
        if which == 1:
            copy.wait_recv()

    copies = exchange_start(1, basis.at[0])
    for it in range(ITERS):
        vec = basis.at[it]
        if it:
            sketch(it, lambda p: vec[p, 0:by, 0:bz])
        exchange_finish(it + 1, vec, copies)

        def scale(p, carry):
            za[p] = vec[p] * dinv[p]
            return carry

        lax.fori_loop(0, X, scale, 0)
        src, dst = za, zb
        for sweep in range(SWEEPS):
            def jacobi(p, carry):
                centre, total = near(src, p)
                dst[p] = (vec[p] + total) * dinv[p]
                return carry

            lax.fori_loop(0, X, jacobi, 0)
            src, dst = dst, src

        def operate(p, carry):
            centre, total = near(src, p)
            inner = centre[0:by, 0:bz]
            value = (6.0 - ksq[p, 0:by, 0:bz]) * inner - total[0:by, 0:bz]
            value = value - SHIFTS[it] * vec[p, 0:by, 0:bz]
            if it == ITERS - 1:
                last[p] = value
            else:
                basis[it + 1, p, 0:by, 0:bz] = value
            return carry

        lax.fori_loop(0, bx if it == ITERS - 1 else X, operate, 0)
        if it < ITERS - 1:
            copies = exchange_start(it + 2, basis.at[it + 1])

        def keep(p, carry):
            pk[it, p] = src[p, 0:by, 0:bz]
            return carry

        lax.fori_loop(0, bx, keep, 0)
    sketch(ITERS, lambda p: last[p])

    lane_r = lax.broadcasted_iota(jnp.int32, (rows, LANES), 1)
    table = jnp.zeros((rows, LANES), jnp.float32)
    for j in range(ITERS + 1):
        table = jnp.where(lane_r == j, jnp.sum(red0[j], axis=1, keepdims=True), table)
    red1[...] = table
    for buf, got, peers, ssem, rsem, out in (
            (red1, got1, plane_peers, rsend1, rrecv1, red2), (red2, got2, z_peers, rsend2, rrecv2, None)):
        sums = []
        for m, peer in enumerate(peers):
            copy = pltpu.make_async_remote_copy(
                src_ref=buf, dst_ref=got.at[m], send_sem=ssem.at[m], recv_sem=rsem.at[m],
                device_id=peer, device_id_type=MESH)
            copy.start()
            sums.append(copy)
        total = buf[...]
        for m, copy in enumerate(sums):
            copy.wait_recv()
            total = total + got[m]
        pending.extend(sums)
        if out is not None:
            out[...] = total
    sketches = []
    for j in range(ITERS + 1):
        column = jnp.sum(jnp.where(lane_r == j, total, 0.0), axis=1, keepdims=True)
        sketches.append(jnp.broadcast_to(column, (rows, LANES)))
    sol, res = small_solve(sketches)
    wide = bz // LANES
    sol = [jnp.concatenate([c] * wide, axis=1) for c in sol]
    res = [jnp.concatenate([c] * wide, axis=1) for c in res]

    def combine(p, carry):
        acc = pk[0, p] * sol[0]
        for i in range(1, ITERS):
            acc = acc + pk[i, p] * sol[i]
        sol_ref[p] = acc
        acc = last[p] * res[ITERS]
        for i in range(ITERS):
            acc = acc + basis[i, p, 0:by, 0:bz] * res[i]
        res_ref[p] = acc
        return carry

    lax.fori_loop(0, bx, combine, 0)
    for which, copy in gathers:
        copy.wait_send()
    for copy in pending:
        copy.wait_send()


def solution(mesh):
    nx, ny, nz = mesh.shape["gx"], mesh.shape["gy"], mesh.shape["gz"]

    def local(right_side, wavenumber_sq, sketch_matrix):
        rows, bx, by, bz = sketch_matrix.shape
        X, Y, Z = nx * bx, by + 2 * DEPTH, bz + LANES
        packed = -(-X * DEPTH // LANES) * LANES
        slots = ITERS + 1
        f32 = jnp.float32
        dma = pltpu.SemaphoreType.DMA
        plane, line = nx * ny - 1, nz - 1
        return pl.pallas_call(
            functools.partial(kernel, (nx, ny, nz)),
            out_shape=(jax.ShapeDtypeStruct((bx, by, bz), f32),) * 2,
            in_specs=[pl.BlockSpec(memory_space=pl.ANY)] * 3,
            out_specs=[pl.BlockSpec(memory_space=pltpu.VMEM)] * 2,
            scratch_shapes=[
                pltpu.VMEM((rows, bx, by, bz), f32),
                pltpu.VMEM((X, Y, Z), f32),
                pltpu.VMEM((X, Y, Z), f32),
                pltpu.VMEM((ITERS, X, Y, Z), f32),
                pltpu.VMEM((bx, by, bz), f32),
                pltpu.VMEM((X, Y, Z), f32),
                pltpu.VMEM((X, Y, Z), f32),
                pltpu.VMEM((ITERS, bx, by, bz), f32),
                pltpu.VMEM((slots, 2, X // 2, 8, bz), f32),
                pltpu.VMEM((slots, 2, X // 2, 8, bz), f32),
                pltpu.VMEM((slots, 2, by, packed), f32),
                pltpu.VMEM((slots, 2, by, packed), f32),
                pltpu.VMEM((slots, 4, 8, packed), f32),
                pltpu.VMEM((slots, rows, LANES), f32),
                pltpu.VMEM((rows, LANES), f32),
                pltpu.VMEM((rows, LANES), f32),
                pltpu.VMEM((plane, rows, LANES), f32),
                pltpu.VMEM((line, rows, LANES), f32),
                dma((3,)),
                dma((2, nx - 1)), dma((2, nx - 1)),
                dma((slots, 8)), dma((slots, 8)),
                dma((plane,)), dma((plane,)),
                dma((line,)), dma((line,)),
            ],
            compiler_params=pltpu.CompilerParams(
                collective_id=0, has_side_effects=True, vmem_limit_bytes=60 * 1024 * 1024),
        )(right_side, wavenumber_sq, sketch_matrix)

    spec = P("gx", "gy", "gz")
    return jax.shard_map(
        local, mesh=mesh, in_specs=(spec, spec, P(None, "gx", "gy", "gz")),
        out_specs=(spec, spec), check_vma=False)
```

```python
import functools

import jax
import jax.numpy as jnp
from jax import lax
from jax.experimental import pallas as pl
from jax.experimental.pallas import tpu as pltpu
from jax.sharding import PartitionSpec as P

SWEEPS = 3
ITERS = 3
DEPTH = SWEEPS + 1
SHIFTS = (0.75, 0.5, 0.25)
MESH = pl.DeviceIdType.MESH
LANES = 128


def planes(count, step, body, carry):
    while count % step:
        step //= 2

    def group(at, carry):
        for i in range(step):
            carry = body(at * step + i, carry)
        return carry

    return lax.fori_loop(0, count // step, group, carry)


def small_solve(sketches):
    def dot(a, b):
        return jnp.sum(a * b, axis=0, keepdims=True)

    beta = jnp.sqrt(dot(sketches[0], sketches[0]))
    combos = [[1.0 / beta]]
    images = [sketches[0] / beta]
    hessen = []
    for it in range(ITERS):
        a = combos[it]
        b = [SHIFTS[i] * a[i] for i in range(it + 1)] + [None]
        for i in range(1, it + 2):
            b[i] = a[i - 1] if b[i] is None else b[i] + a[i - 1]
        s = b[0] * sketches[0]
        for i in range(1, it + 2):
            s = s + b[i] * sketches[i]
        c = [dot(images[i], s) for i in range(it + 1)]
        t = s
        for i in range(it + 1):
            t = t - c[i] * images[i]
            for m in range(i + 1):
                b[m] = b[m] - c[i] * combos[i][m]
        nu = jnp.sqrt(dot(t, t))
        images.append(t / nu)
        combos.append([x / nu for x in b])
        hessen.append(c + [nu])

    def vdot(a, b):
        total = a[0] * b[0]
        for i in range(1, min(len(a), len(b))):
            total = total + a[i] * b[i]
        return total

    basis, upper = [], [[None] * ITERS for _ in range(ITERS)]
    for col in range(ITERS):
        column = list(hessen[col])
        for row in range(col):
            factor = vdot(basis[row], column)
            upper[row][col] = factor
            for i in range(len(basis[row])):
                column[i] = column[i] - factor * basis[row][i]
        norm = jnp.sqrt(vdot(column, column))
        upper[col][col] = norm
        basis.append([x / norm for x in column])
    y = [None] * ITERS
    for row in reversed(range(ITERS)):
        acc = basis[row][0] * beta
        for col in range(row + 1, ITERS):
            acc = acc - upper[row][col] * y[col]
        y[row] = acc / upper[row][row]
    e = []
    for i in range(ITERS + 1):
        acc = beta if i == 0 else jnp.zeros_like(beta)
        for col in range(ITERS):
            if i <= col + 1:
                acc = acc - hessen[col][i] * y[col]
        e.append(acc)
    sol, res = [], []
    for i in range(ITERS):
        acc = y[i] * combos[i][i]
        for j in range(i + 1, ITERS):
            acc = acc + y[j] * combos[j][i]
        sol.append(acc)
    for i in range(ITERS + 1):
        acc = e[i] * combos[i][i]
        for j in range(i + 1, ITERS + 1):
            acc = acc + e[j] * combos[j][i]
        res.append(acc)
    return sol, res


def kernel(sizes, r_ref, k_ref, s_ref, sol_ref, res_ref,
           sk, ksq, dinv, basis, last, za, zb, pk,
           ysend, yrecv, zsend, zrecv, crecv, red0, red1, red2, got1, got2,
           local_sem, gsend, grecv, xsend, xrecv, rsend1, rrecv1, rsend2, rrecv2):
    nx, ny, nz = sizes
    bx, by, bz = r_ref.shape
    rows = sk.shape[0]
    X, Y, Z = nx * bx, by + 2 * DEPTH, bz + LANES
    half = X // 2
    per = LANES // DEPTH
    groups = zsend.shape[-1] // LANES
    gx, gy, gz = lax.axis_index("gx"), lax.axis_index("gy"), lax.axis_index("gz")

    def wrap(i, n):
        return lax.rem(i + n, n)

    py, qy = wrap(gy - 1, ny), wrap(gy + 1, ny)
    pz, qz = wrap(gz - 1, nz), wrap(gz + 1, nz)

    plane_peers = []
    for dx in range(nx):
        for dy in range(ny):
            if dx or dy:
                plane_peers.append((wrap(gx + dx, nx), wrap(gy + dy, ny), gz))
    z_peers = [(gx, gy, wrap(gz + d, nz)) for d in range(1, nz)]
    diagonals = [(gx, py, pz), (gx, qy, pz), (gx, py, qz), (gx, qy, qz)]

    own_s = pltpu.make_async_copy(s_ref, sk, local_sem.at[0])
    own_k = pltpu.make_async_copy(
        k_ref, ksq.at[pl.ds(0, bx), pl.ds(0, by), pl.ds(0, bz)], local_sem.at[1])
    own_r = pltpu.make_async_copy(
        r_ref, basis.at[0, pl.ds(0, bx), pl.ds(0, by), pl.ds(0, bz)], local_sem.at[2])
    own_k.start()
    own_r.start()
    own_s.start()

    barrier = pltpu.get_barrier_semaphore()
    everyone = plane_peers + z_peers + diagonals
    for peer in everyone:
        pl.semaphore_signal(barrier, inc=1, device_id=peer, device_id_type=MESH)
    pl.semaphore_wait(barrier, len(everyone))

    gathers = []
    for which, src in ((0, k_ref), (1, r_ref)):
        for i in range(1, nx):
            dst = ksq if which == 0 else basis.at[0]
            copy = pltpu.make_async_remote_copy(
                src_ref=src,
                dst_ref=dst.at[pl.ds(i * bx, bx), pl.ds(0, by), pl.ds(0, bz)],
                send_sem=gsend.at[which, i - 1], recv_sem=grecv.at[which, i - 1],
                device_id=(wrap(gx - i, nx), gy, gz), device_id_type=MESH)
            copy.start()
            gathers.append((which, copy))

    sub_low = lax.broadcasted_iota(jnp.int32, (8, bz), 0) < DEPTH
    sub_low_z = lax.broadcasted_iota(jnp.int32, (8, zsend.shape[-1]), 0) < DEPTH
    lane_by = lax.broadcasted_iota(jnp.int32, (by, LANES), 1)
    lane_y = lax.broadcasted_iota(jnp.int32, (Y, LANES), 1)

    pending = []

    def exchange_start(slot, buf):
        def pack_y(p, carry):
            low0, low1 = buf[p, 0:8, 0:bz], buf[p + half, 0:8, 0:bz]
            high0, high1 = buf[p, by - 8:by, 0:bz], buf[p + half, by - 8:by, 0:bz]
            ysend[slot, 0, p] = jnp.where(sub_low, low0, pltpu.roll(low1, DEPTH, 0))
            ysend[slot, 1, p] = jnp.where(sub_low, pltpu.roll(high0, DEPTH, 0), high1)
            return carry

        planes(half, 4, pack_y, 0)
        copies = []

        def send(m, src, dst, peer):
            copy = pltpu.make_async_remote_copy(
                src_ref=src, dst_ref=dst, send_sem=xsend.at[slot, m], recv_sem=xrecv.at[slot, m],
                device_id=peer, device_id_type=MESH)
            copy.start()
            copies.append(copy)

        send(0, ysend.at[slot, 0], yrecv.at[slot, 0], (gx, py, gz))
        send(1, ysend.at[slot, 1], yrecv.at[slot, 1], (gx, qy, gz))
        for g in range(groups):
            def pack_z(p, carry):
                left, right = carry
                plane = g * per + p
                mine = lax.div(lane_by, DEPTH) == p
                first = pltpu.roll(buf[plane, 0:by, 0:LANES], DEPTH * p, 1)
                final = pltpu.roll(
                    buf[plane, 0:by, bz - LANES:bz], lax.rem(DEPTH * (p + 1), LANES), 1)
                return jnp.where(mine, first, left), jnp.where(mine, final, right)

            zero = jnp.zeros((by, LANES), jnp.float32)
            left, right = planes(min(per, X - g * per), 8, pack_z, (zero, zero))
            zsend[slot, 0, :, g * LANES:(g + 1) * LANES] = left
            zsend[slot, 1, :, g * LANES:(g + 1) * LANES] = right
        send(2, zsend.at[slot, 0], zrecv.at[slot, 0], (gx, gy, pz))
        send(3, zsend.at[slot, 1], zrecv.at[slot, 1], (gx, gy, qz))
        for m, (side, row, peer) in enumerate((
                (0, 0, (gx, py, pz)), (0, by - 8, (gx, qy, pz)),
                (1, 0, (gx, py, qz)), (1, by - 8, (gx, qy, qz)))):
            send(4 + m, zsend.at[slot, side, pl.ds(row, 8)], crecv.at[slot, m], peer)
        pending.extend(copies)
        return copies

    def exchange_finish(slot, buf, copies):
        copies[0].wait_recv()
        copies[1].wait_recv()

        def unpack_y(p, carry):
            up, down = yrecv[slot, 0, p], yrecv[slot, 1, p]
            buf[p, by:Y, 0:bz] = jnp.where(sub_low, up, pltpu.roll(down, DEPTH, 0))
            buf[p + half, by:Y, 0:bz] = jnp.where(sub_low, pltpu.roll(up, DEPTH, 0), down)
            return carry

        planes(half, 4, unpack_y, 0)
        for copy in copies[2:]:
            copy.wait_recv()
        right = jnp.concatenate(
            [zrecv[slot, 0], jnp.where(sub_low_z, crecv[slot, 0], crecv[slot, 1])], axis=0)
        left = jnp.concatenate(
            [zrecv[slot, 1], jnp.where(sub_low_z, crecv[slot, 2], crecv[slot, 3])], axis=0)
        for g in range(groups):
            right_g = right[:, g * LANES:(g + 1) * LANES]
            left_g = left[:, g * LANES:(g + 1) * LANES]

            def unpack_z(p, carry):
                high = pltpu.roll(right_g, lax.rem(LANES - DEPTH * p, LANES), 1)
                low = pltpu.roll(left_g, LANES - DEPTH - DEPTH * p, 1)
                tile = jnp.where(
                    lane_y < DEPTH, high, jnp.where(lane_y >= LANES - DEPTH, low, 0.0))
                buf[g * per + p, :, bz:Z] = tile
                return carry

            planes(min(per, X - g * per), 8, unpack_z, 0)

    def near(z_ref, p):
        centre = z_ref[p]
        total = z_ref[lax.rem(p + X - 1, X)] + z_ref[lax.rem(p + 1, X)]
        total = total + pltpu.roll(centre, 1, 0) + pltpu.roll(centre, Y - 1, 0)
        total = total + pltpu.roll(centre, 1, 1) + pltpu.roll(centre, Z - 1, 1)
        return centre, total

    def sketch(slot, plane_of):
        def body(p, acc):
            v = plane_of(p)
            out = []
            for row in range(rows):
                prod = sk[row, p] * v
                part = prod[:, 0:LANES]
                for i in range(1, bz // LANES):
                    part = part + prod[:, i * LANES:(i + 1) * LANES]
                tile = part[0:8]
                for i in range(1, by // 8):
                    tile = tile + part[8 * i:8 * i + 8]
                out.append(acc[row] + tile)
            return tuple(out)

        acc = lax.fori_loop(0, bx, body, tuple(jnp.zeros((8, LANES), jnp.float32) for _ in range(rows)))
        for row in range(rows):
            red0[slot, pl.ds(row, 1)] = jnp.sum(acc[row], axis=0, keepdims=True)

    own_k.wait()
    for which, copy in gathers:
        if which == 0:
            copy.wait_recv()
    k_copies = exchange_start(0, ksq)
    own_r.wait()
    own_s.wait()
    sketch(0, lambda p: basis[0, p, 0:by, 0:bz])
    for which, copy in gathers:
        if which == 1:
            copy.wait_recv()
    copies = exchange_start(1, basis.at[0])
    exchange_finish(0, ksq, k_copies)

    def invert(p, carry):
        dinv[p] = 1.0 / (6.0 + ksq[p])
        return carry

    planes(X, 4, invert, 0)
    for it in range(ITERS):
        vec = basis.at[it]
        if it:
            sketch(it, lambda p: vec[p, 0:by, 0:bz])
        exchange_finish(it + 1, vec, copies)

        def scale(p, carry):
            za[p] = vec[p] * dinv[p]
            return carry

        planes(X, 4, scale, 0)
        src, dst = za, zb
        for sweep in range(SWEEPS):
            reach = SWEEPS - sweep
            shrunk = it == ITERS - 1 and bx + 2 * reach < X
            begin, count = (X - reach, bx + 2 * reach) if shrunk else (0, X)

            def jacobi(at, carry):
                where = [lax.rem(begin + 2 * at + i, X) for i in range(2)]
                values = []
                for p in where:
                    centre, total = near(src, p)
                    values.append((vec[p] + total) * dinv[p])
                for p, value in zip(where, values):
                    dst[p] = value
                return carry

            lax.fori_loop(0, count // 2, jacobi, 0)
            src, dst = dst, src

        def operate(p, carry):
            centre, total = near(src, p)
            inner = centre[0:by, 0:bz]
            value = (6.0 - ksq[p, 0:by, 0:bz]) * inner - total[0:by, 0:bz]
            value = value - SHIFTS[it] * vec[p, 0:by, 0:bz]
            if it == ITERS - 1:
                last[p] = value
            else:
                basis[it + 1, p, 0:by, 0:bz] = value
            return carry

        planes(bx if it == ITERS - 1 else X, 2, operate, 0)
        if it < ITERS - 1:
            copies = exchange_start(it + 2, basis.at[it + 1])

        def keep(p, carry):
            pk[it, p] = src[p, 0:by, 0:bz]
            return carry

        planes(bx, 4, keep, 0)
    sketch(ITERS, lambda p: last[p])

    lane_r = lax.broadcasted_iota(jnp.int32, (rows, LANES), 1)
    table = jnp.zeros((rows, LANES), jnp.float32)
    for j in range(ITERS + 1):
        table = jnp.where(lane_r == j, jnp.sum(red0[j], axis=1, keepdims=True), table)
    red1[...] = table
    for buf, got, peers, ssem, rsem, out in (
            (red1, got1, plane_peers, rsend1, rrecv1, red2), (red2, got2, z_peers, rsend2, rrecv2, None)):
        sums = []
        for m, peer in enumerate(peers):
            copy = pltpu.make_async_remote_copy(
                src_ref=buf, dst_ref=got.at[m], send_sem=ssem.at[m], recv_sem=rsem.at[m],
                device_id=peer, device_id_type=MESH)
            copy.start()
            sums.append(copy)
        total = buf[...]
        for m, copy in enumerate(sums):
            copy.wait_recv()
            total = total + got[m]
        pending.extend(sums)
        if out is not None:
            out[...] = total
    sketches = []
    for j in range(ITERS + 1):
        column = jnp.sum(jnp.where(lane_r == j, total, 0.0), axis=1, keepdims=True)
        sketches.append(jnp.broadcast_to(column, (rows, LANES)))
    sol, res = small_solve(sketches)
    wide = bz // LANES
    sol = [jnp.concatenate([c] * wide, axis=1) for c in sol]
    res = [jnp.concatenate([c] * wide, axis=1) for c in res]

    def combine(p, carry):
        acc = pk[0, p] * sol[0]
        for i in range(1, ITERS):
            acc = acc + pk[i, p] * sol[i]
        sol_ref[p] = acc
        acc = last[p] * res[ITERS]
        for i in range(ITERS):
            acc = acc + basis[i, p, 0:by, 0:bz] * res[i]
        res_ref[p] = acc
        return carry

    planes(bx, 2, combine, 0)
    for which, copy in gathers:
        copy.wait_send()
    for copy in pending:
        copy.wait_send()


def write_out(a_ref, b_ref, sol_ref, res_ref):
    sol_ref[...] = a_ref[...]
    res_ref[...] = b_ref[...]


def solution(mesh):
    nx, ny, nz = mesh.shape["gx"], mesh.shape["gy"], mesh.shape["gz"]

    def local(right_side, wavenumber_sq, sketch_matrix):
        rows, bx, by, bz = sketch_matrix.shape
        X, Y, Z = nx * bx, by + 2 * DEPTH, bz + LANES
        packed = -(-X * DEPTH // LANES) * LANES
        slots = ITERS + 1
        f32 = jnp.float32
        dma = pltpu.SemaphoreType.DMA
        plane, line = nx * ny - 1, nz - 1
        found = pl.pallas_call(
            functools.partial(kernel, (nx, ny, nz)),
            out_shape=(jax.ShapeDtypeStruct((bx, by, bz), f32),) * 2,
            in_specs=[pl.BlockSpec(memory_space=pl.ANY)] * 3,
            out_specs=[pl.BlockSpec(memory_space=pltpu.VMEM)] * 2,
            scratch_shapes=[
                pltpu.VMEM((rows, bx, by, bz), f32),
                pltpu.VMEM((X, Y, Z), f32),
                pltpu.VMEM((X, Y, Z), f32),
                pltpu.VMEM((ITERS, X, Y, Z), f32),
                pltpu.VMEM((bx, by, bz), f32),
                pltpu.VMEM((X, Y, Z), f32),
                pltpu.VMEM((X, Y, Z), f32),
                pltpu.VMEM((ITERS, bx, by, bz), f32),
                pltpu.VMEM((slots, 2, X // 2, 8, bz), f32),
                pltpu.VMEM((slots, 2, X // 2, 8, bz), f32),
                pltpu.VMEM((slots, 2, by, packed), f32),
                pltpu.VMEM((slots, 2, by, packed), f32),
                pltpu.VMEM((slots, 4, 8, packed), f32),
                pltpu.VMEM((slots, rows, LANES), f32),
                pltpu.VMEM((rows, LANES), f32),
                pltpu.VMEM((rows, LANES), f32),
                pltpu.VMEM((plane, rows, LANES), f32),
                pltpu.VMEM((line, rows, LANES), f32),
                dma((3,)),
                dma((2, nx - 1)), dma((2, nx - 1)),
                dma((slots, 8)), dma((slots, 8)),
                dma((plane,)), dma((plane,)),
                dma((line,)), dma((line,)),
            ],
            compiler_params=pltpu.CompilerParams(
                collective_id=0, has_side_effects=True, vmem_limit_bytes=60 * 1024 * 1024),
        )(right_side, wavenumber_sq, sketch_matrix)
        return pl.pallas_call(
            write_out,
            out_shape=(jax.ShapeDtypeStruct((bx, by, bz), f32),) * 2,
            in_specs=[pl.BlockSpec(memory_space=pltpu.VMEM)] * 2,
            out_specs=[pl.BlockSpec(memory_space=pltpu.VMEM)] * 2,
        )(*found)

    spec = P("gx", "gy", "gz")
    return jax.shard_map(
        local, mesh=mesh, in_specs=(spec, spec, P(None, "gx", "gy", "gz")),
        out_specs=(spec, spec), check_vma=False)
```

```python
import functools

import jax
import jax.numpy as jnp
from jax import lax
from jax.experimental import pallas as pl
from jax.experimental.pallas import tpu as pltpu
from jax.sharding import PartitionSpec as P

SWEEPS = 3
ITERS = 3
DEPTH = SWEEPS + 1
SHIFTS = (0.75, 0.5, 0.25)
MESH = pl.DeviceIdType.MESH
LANES = 128


def planes(count, step, body, carry):
    while count % step:
        step //= 2

    def group(at, carry):
        for i in range(step):
            carry = body(at * step + i, carry)
        return carry

    return lax.fori_loop(0, count // step, group, carry)


def small_solve(sketches):
    def dot(a, b):
        return jnp.sum(a * b, axis=0, keepdims=True)

    beta = jnp.sqrt(dot(sketches[0], sketches[0]))
    combos = [[1.0 / beta]]
    images = [sketches[0] / beta]
    hessen = []
    for it in range(ITERS):
        a = combos[it]
        b = [SHIFTS[i] * a[i] for i in range(it + 1)] + [None]
        for i in range(1, it + 2):
            b[i] = a[i - 1] if b[i] is None else b[i] + a[i - 1]
        s = b[0] * sketches[0]
        for i in range(1, it + 2):
            s = s + b[i] * sketches[i]
        c = [dot(images[i], s) for i in range(it + 1)]
        t = s
        for i in range(it + 1):
            t = t - c[i] * images[i]
            for m in range(i + 1):
                b[m] = b[m] - c[i] * combos[i][m]
        nu = jnp.sqrt(dot(t, t))
        images.append(t / nu)
        combos.append([x / nu for x in b])
        hessen.append(c + [nu])

    def vdot(a, b):
        total = a[0] * b[0]
        for i in range(1, min(len(a), len(b))):
            total = total + a[i] * b[i]
        return total

    basis, upper = [], [[None] * ITERS for _ in range(ITERS)]
    for col in range(ITERS):
        column = list(hessen[col])
        for row in range(col):
            factor = vdot(basis[row], column)
            upper[row][col] = factor
            for i in range(len(basis[row])):
                column[i] = column[i] - factor * basis[row][i]
        norm = jnp.sqrt(vdot(column, column))
        upper[col][col] = norm
        basis.append([x / norm for x in column])
    y = [None] * ITERS
    for row in reversed(range(ITERS)):
        acc = basis[row][0] * beta
        for col in range(row + 1, ITERS):
            acc = acc - upper[row][col] * y[col]
        y[row] = acc / upper[row][row]
    e = []
    for i in range(ITERS + 1):
        acc = beta if i == 0 else jnp.zeros_like(beta)
        for col in range(ITERS):
            if i <= col + 1:
                acc = acc - hessen[col][i] * y[col]
        e.append(acc)
    sol, res = [], []
    for i in range(ITERS):
        acc = y[i] * combos[i][i]
        for j in range(i + 1, ITERS):
            acc = acc + y[j] * combos[j][i]
        sol.append(acc)
    for i in range(ITERS + 1):
        acc = e[i] * combos[i][i]
        for j in range(i + 1, ITERS + 1):
            acc = acc + e[j] * combos[j][i]
        res.append(acc)
    return sol, res


def kernel(sizes, r_ref, k_ref, s_ref, sol_ref, res_ref,
           sk, ksq, dinv, basis, last, za, zb, pk,
           ysend, yrecv, zsend, zrecv, crecv, red0, red1, red2, got1, got2,
           local_sem, gsend, grecv, xsend, xrecv, rsend1, rrecv1, rsend2, rrecv2):
    nx, ny, nz = sizes
    bx, by, bz = r_ref.shape
    rows = sk.shape[0]
    X, Y, Z = nx * bx, by + 2 * DEPTH, bz + LANES
    half = X // 2
    per = LANES // DEPTH
    groups = zsend.shape[-1] // LANES
    gx, gy, gz = lax.axis_index("gx"), lax.axis_index("gy"), lax.axis_index("gz")

    def wrap(i, n):
        return lax.rem(i + n, n)

    py, qy = wrap(gy - 1, ny), wrap(gy + 1, ny)
    pz, qz = wrap(gz - 1, nz), wrap(gz + 1, nz)

    plane_peers = []
    for dx in range(nx):
        for dy in range(ny):
            if dx or dy:
                plane_peers.append((wrap(gx + dx, nx), wrap(gy + dy, ny), gz))
    z_peers = [(gx, gy, wrap(gz + d, nz)) for d in range(1, nz)]
    diagonals = [(gx, py, pz), (gx, qy, pz), (gx, py, qz), (gx, qy, qz)]

    own_s = pltpu.make_async_copy(s_ref, sk, local_sem.at[0])
    own_k = pltpu.make_async_copy(
        k_ref, ksq.at[pl.ds(0, bx), pl.ds(0, by), pl.ds(0, bz)], local_sem.at[1])
    own_r = pltpu.make_async_copy(
        r_ref, basis.at[0, pl.ds(0, bx), pl.ds(0, by), pl.ds(0, bz)], local_sem.at[2])
    own_k.start()
    own_r.start()
    own_s.start()

    barrier = pltpu.get_barrier_semaphore()
    everyone = plane_peers + z_peers + diagonals
    for peer in everyone:
        pl.semaphore_signal(barrier, inc=1, device_id=peer, device_id_type=MESH)
    pl.semaphore_wait(barrier, len(everyone))

    gathers = []
    for which, src in ((0, k_ref), (1, r_ref)):
        for i in range(1, nx):
            dst = ksq if which == 0 else basis.at[0]
            copy = pltpu.make_async_remote_copy(
                src_ref=src,
                dst_ref=dst.at[pl.ds(i * bx, bx), pl.ds(0, by), pl.ds(0, bz)],
                send_sem=gsend.at[which, i - 1], recv_sem=grecv.at[which, i - 1],
                device_id=(wrap(gx - i, nx), gy, gz), device_id_type=MESH)
            copy.start()
            gathers.append((which, copy))

    sub_low = lax.broadcasted_iota(jnp.int32, (8, bz), 0) < DEPTH
    sub_low_z = lax.broadcasted_iota(jnp.int32, (8, zsend.shape[-1]), 0) < DEPTH
    lane_by = lax.broadcasted_iota(jnp.int32, (by, LANES), 1)
    lane_y = lax.broadcasted_iota(jnp.int32, (Y, LANES), 1)

    pending = []

    def exchange_start(slot, buf):
        def pack_y(p, carry):
            low0, low1 = buf[p, 0:8, 0:bz], buf[p + half, 0:8, 0:bz]
            high0, high1 = buf[p, by - 8:by, 0:bz], buf[p + half, by - 8:by, 0:bz]
            ysend[slot, 0, p] = jnp.where(sub_low, low0, pltpu.roll(low1, DEPTH, 0))
            ysend[slot, 1, p] = jnp.where(sub_low, pltpu.roll(high0, DEPTH, 0), high1)
            return carry

        planes(half, 4, pack_y, 0)
        copies = []

        def send(m, src, dst, peer):
            copy = pltpu.make_async_remote_copy(
                src_ref=src, dst_ref=dst, send_sem=xsend.at[slot, m], recv_sem=xrecv.at[slot, m],
                device_id=peer, device_id_type=MESH)
            copy.start()
            copies.append(copy)

        send(0, ysend.at[slot, 0], yrecv.at[slot, 0], (gx, py, gz))
        send(1, ysend.at[slot, 1], yrecv.at[slot, 1], (gx, qy, gz))
        for g in range(groups):
            def pack_z(p, carry):
                left, right = carry
                plane = g * per + p
                mine = lax.div(lane_by, DEPTH) == p
                first = pltpu.roll(buf[plane, 0:by, 0:LANES], DEPTH * p, 1)
                final = pltpu.roll(
                    buf[plane, 0:by, bz - LANES:bz], lax.rem(DEPTH * (p + 1), LANES), 1)
                return jnp.where(mine, first, left), jnp.where(mine, final, right)

            zero = jnp.zeros((by, LANES), jnp.float32)
            left, right = planes(min(per, X - g * per), 8, pack_z, (zero, zero))
            zsend[slot, 0, :, g * LANES:(g + 1) * LANES] = left
            zsend[slot, 1, :, g * LANES:(g + 1) * LANES] = right
        send(2, zsend.at[slot, 0], zrecv.at[slot, 0], (gx, gy, pz))
        send(3, zsend.at[slot, 1], zrecv.at[slot, 1], (gx, gy, qz))
        for m, (side, row, peer) in enumerate((
                (0, 0, (gx, py, pz)), (0, by - 8, (gx, qy, pz)),
                (1, 0, (gx, py, qz)), (1, by - 8, (gx, qy, qz)))):
            send(4 + m, zsend.at[slot, side, pl.ds(row, 8)], crecv.at[slot, m], peer)
        pending.extend(copies)
        return copies

    def exchange_finish(slot, buf, copies):
        copies[0].wait_recv()
        copies[1].wait_recv()

        def unpack_y(p, carry):
            up, down = yrecv[slot, 0, p], yrecv[slot, 1, p]
            buf[p, by:Y, 0:bz] = jnp.where(sub_low, up, pltpu.roll(down, DEPTH, 0))
            buf[p + half, by:Y, 0:bz] = jnp.where(sub_low, pltpu.roll(up, DEPTH, 0), down)
            return carry

        planes(half, 4, unpack_y, 0)
        for copy in copies[2:]:
            copy.wait_recv()
        right = jnp.concatenate(
            [zrecv[slot, 0], jnp.where(sub_low_z, crecv[slot, 0], crecv[slot, 1])], axis=0)
        left = jnp.concatenate(
            [zrecv[slot, 1], jnp.where(sub_low_z, crecv[slot, 2], crecv[slot, 3])], axis=0)
        for g in range(groups):
            right_g = right[:, g * LANES:(g + 1) * LANES]
            left_g = left[:, g * LANES:(g + 1) * LANES]

            def unpack_z(p, carry):
                high = pltpu.roll(right_g, lax.rem(LANES - DEPTH * p, LANES), 1)
                low = pltpu.roll(left_g, LANES - DEPTH - DEPTH * p, 1)
                tile = jnp.where(
                    lane_y < DEPTH, high, jnp.where(lane_y >= LANES - DEPTH, low, 0.0))
                buf[g * per + p, :, bz:Z] = tile
                return carry

            planes(min(per, X - g * per), 8, unpack_z, 0)

    def near(z_ref, p):
        centre = z_ref[p]
        total = z_ref[lax.rem(p + X - 1, X)] + z_ref[lax.rem(p + 1, X)]
        total = total + pltpu.roll(centre, 1, 0) + pltpu.roll(centre, Y - 1, 0)
        total = total + pltpu.roll(centre, 1, 1) + pltpu.roll(centre, Z - 1, 1)
        return centre, total

    def sketch(slot, plane_of):
        def body(p, acc):
            v = plane_of(p)
            out = []
            for row in range(rows):
                prod = sk[row, p] * v
                part = prod[:, 0:LANES]
                for i in range(1, bz // LANES):
                    part = part + prod[:, i * LANES:(i + 1) * LANES]
                tile = part[0:8]
                for i in range(1, by // 8):
                    tile = tile + part[8 * i:8 * i + 8]
                out.append(acc[row] + tile)
            return tuple(out)

        acc = planes(bx, 2, body, tuple(jnp.zeros((8, LANES), jnp.float32) for _ in range(rows)))
        for row in range(rows):
            red0[slot, pl.ds(row, 1)] = jnp.sum(acc[row], axis=0, keepdims=True)

    own_k.wait()
    for which, copy in gathers:
        if which == 0:
            copy.wait_recv()
    k_copies = exchange_start(0, ksq)
    own_r.wait()
    own_s.wait()
    sketch(0, lambda p: basis[0, p, 0:by, 0:bz])
    for which, copy in gathers:
        if which == 1:
            copy.wait_recv()
    copies = exchange_start(1, basis.at[0])
    exchange_finish(0, ksq, k_copies)

    def invert(p, carry):
        dinv[p] = 1.0 / (6.0 + ksq[p])
        return carry

    planes(X, 4, invert, 0)
    for it in range(ITERS):
        vec = basis.at[it]
        if it:
            sketch(it, lambda p: vec[p, 0:by, 0:bz])
        exchange_finish(it + 1, vec, copies)

        def scale(p, carry):
            za[p] = vec[p] * dinv[p]
            return carry

        planes(X, 4, scale, 0)
        src, dst = za, zb
        for sweep in range(SWEEPS):
            reach = SWEEPS - sweep
            shrunk = it == ITERS - 1 and bx + 2 * reach < X
            begin, count = (X - reach, bx + 2 * reach) if shrunk else (0, X)

            step = 4 if count % 4 == 0 else 2

            def jacobi(at, carry):
                where = [lax.rem(begin + step * at + i, X) for i in range(step)]
                values = []
                for p in where:
                    centre, total = near(src, p)
                    values.append((vec[p] + total) * dinv[p])
                for p, value in zip(where, values):
                    dst[p] = value
                return carry

            lax.fori_loop(0, count // step, jacobi, 0)
            src, dst = dst, src

        def operate(at, carry):
            values = []
            for i in range(4):
                p = 4 * at + i
                centre, total = near(src, p)
                inner = centre[0:by, 0:bz]
                value = (6.0 - ksq[p, 0:by, 0:bz]) * inner - total[0:by, 0:bz]
                values.append(value - SHIFTS[it] * vec[p, 0:by, 0:bz])
            for i, value in enumerate(values):
                if it == ITERS - 1:
                    last[4 * at + i] = value
                else:
                    basis[it + 1, 4 * at + i, 0:by, 0:bz] = value
            return carry

        lax.fori_loop(0, (bx if it == ITERS - 1 else X) // 4, operate, 0)
        if it < ITERS - 1:
            copies = exchange_start(it + 2, basis.at[it + 1])

        def keep(p, carry):
            pk[it, p] = src[p, 0:by, 0:bz]
            return carry

        planes(bx, 4, keep, 0)
    sketch(ITERS, lambda p: last[p])

    lane_r = lax.broadcasted_iota(jnp.int32, (8, LANES), 1)
    table = jnp.zeros((8, LANES), jnp.float32)
    parts = rows // 8
    for j in range(ITERS + 1):
        for h in range(parts):
            table = jnp.where(
                lane_r == j * parts + h,
                jnp.sum(red0[j, pl.ds(8 * h, 8)], axis=1, keepdims=True), table)
    red1[...] = table
    for buf, got, peers, ssem, rsem, out in (
            (red1, got1, plane_peers, rsend1, rrecv1, red2), (red2, got2, z_peers, rsend2, rrecv2, None)):
        sums = []
        for m, peer in enumerate(peers):
            copy = pltpu.make_async_remote_copy(
                src_ref=buf, dst_ref=got.at[m], send_sem=ssem.at[m], recv_sem=rsem.at[m],
                device_id=peer, device_id_type=MESH)
            copy.start()
            sums.append(copy)
        total = buf[...]
        for m, copy in enumerate(sums):
            copy.wait_recv()
            total = total + got[m]
        pending.extend(sums)
        if out is not None:
            out[...] = total
    sketches = []
    for j in range(ITERS + 1):
        sketches.append(jnp.concatenate([
            jnp.broadcast_to(jnp.sum(
                jnp.where(lane_r == j * parts + h, total, 0.0), axis=1, keepdims=True), (8, LANES))
            for h in range(parts)], axis=0))
    sol, res = small_solve(sketches)
    wide = bz // LANES
    sol = [jnp.concatenate([c] * wide, axis=1) for c in sol]
    res = [jnp.concatenate([c] * wide, axis=1) for c in res]

    def combine(p, carry):
        acc = pk[0, p] * sol[0]
        for i in range(1, ITERS):
            acc = acc + pk[i, p] * sol[i]
        sol_ref[p] = acc
        acc = last[p] * res[ITERS]
        for i in range(ITERS):
            acc = acc + basis[i, p, 0:by, 0:bz] * res[i]
        res_ref[p] = acc
        return carry

    planes(bx, 2, combine, 0)
    for which, copy in gathers:
        copy.wait_send()
    for copy in pending:
        copy.wait_send()


def write_out(a_ref, b_ref, sol_ref, res_ref):
    sol_ref[...] = a_ref[...]
    res_ref[...] = b_ref[...]


def solution(mesh):
    nx, ny, nz = mesh.shape["gx"], mesh.shape["gy"], mesh.shape["gz"]

    def local(right_side, wavenumber_sq, sketch_matrix):
        rows, bx, by, bz = sketch_matrix.shape
        X, Y, Z = nx * bx, by + 2 * DEPTH, bz + LANES
        packed = -(-X * DEPTH // LANES) * LANES
        slots = ITERS + 1
        f32 = jnp.float32
        dma = pltpu.SemaphoreType.DMA
        plane, line = nx * ny - 1, nz - 1
        found = pl.pallas_call(
            functools.partial(kernel, (nx, ny, nz)),
            out_shape=(jax.ShapeDtypeStruct((bx, by, bz), f32),) * 2,
            in_specs=[pl.BlockSpec(memory_space=pl.ANY)] * 3,
            out_specs=[pl.BlockSpec(memory_space=pltpu.VMEM)] * 2,
            scratch_shapes=[
                pltpu.VMEM((rows, bx, by, bz), f32),
                pltpu.VMEM((X, Y, Z), f32),
                pltpu.VMEM((X, Y, Z), f32),
                pltpu.VMEM((ITERS, X, Y, Z), f32),
                pltpu.VMEM((bx, by, bz), f32),
                pltpu.VMEM((X, Y, Z), f32),
                pltpu.VMEM((X, Y, Z), f32),
                pltpu.VMEM((ITERS, bx, by, bz), f32),
                pltpu.VMEM((slots, 2, X // 2, 8, bz), f32),
                pltpu.VMEM((slots, 2, X // 2, 8, bz), f32),
                pltpu.VMEM((slots, 2, by, packed), f32),
                pltpu.VMEM((slots, 2, by, packed), f32),
                pltpu.VMEM((slots, 4, 8, packed), f32),
                pltpu.VMEM((slots, rows, LANES), f32),
                pltpu.VMEM((8, LANES), f32),
                pltpu.VMEM((8, LANES), f32),
                pltpu.VMEM((plane, 8, LANES), f32),
                pltpu.VMEM((line, 8, LANES), f32),
                dma((3,)),
                dma((2, nx - 1)), dma((2, nx - 1)),
                dma((slots, 8)), dma((slots, 8)),
                dma((plane,)), dma((plane,)),
                dma((line,)), dma((line,)),
            ],
            compiler_params=pltpu.CompilerParams(
                collective_id=0, has_side_effects=True, vmem_limit_bytes=60 * 1024 * 1024),
        )(right_side, wavenumber_sq, sketch_matrix)
        return pl.pallas_call(
            write_out,
            out_shape=(jax.ShapeDtypeStruct((bx, by, bz), f32),) * 2,
            in_specs=[pl.BlockSpec(memory_space=pltpu.VMEM)] * 2,
            out_specs=[pl.BlockSpec(memory_space=pltpu.VMEM)] * 2,
        )(*found)

    spec = P("gx", "gy", "gz")
    return jax.shard_map(
        local, mesh=mesh, in_specs=(spec, spec, P(None, "gx", "gy", "gz")),
        out_specs=(spec, spec), check_vma=False)
```

```python
import functools

import jax
import jax.numpy as jnp
from jax import lax
from jax.experimental import pallas as pl
from jax.experimental.pallas import tpu as pltpu
from jax.sharding import PartitionSpec as P

SWEEPS = 3
ITERS = 3
DEPTH = SWEEPS + 1
SHIFTS = (0.75, 0.5, 0.25)
MESH = pl.DeviceIdType.MESH
LANES = 128


def planes(count, step, body, carry):
    while count % step:
        step //= 2

    def group(at, carry):
        for i in range(step):
            carry = body(at * step + i, carry)
        return carry

    return lax.fori_loop(0, count // step, group, carry)


def small_solve(sketches):
    def dot(a, b):
        return jnp.sum(a * b, axis=0, keepdims=True)

    beta = jnp.sqrt(dot(sketches[0], sketches[0]))
    combos = [[1.0 / beta]]
    images = [sketches[0] / beta]
    hessen = []
    for it in range(ITERS):
        a = combos[it]
        b = [SHIFTS[i] * a[i] for i in range(it + 1)] + [None]
        for i in range(1, it + 2):
            b[i] = a[i - 1] if b[i] is None else b[i] + a[i - 1]
        s = b[0] * sketches[0]
        for i in range(1, it + 2):
            s = s + b[i] * sketches[i]
        c = [dot(images[i], s) for i in range(it + 1)]
        t = s
        for i in range(it + 1):
            t = t - c[i] * images[i]
            for m in range(i + 1):
                b[m] = b[m] - c[i] * combos[i][m]
        nu = jnp.sqrt(dot(t, t))
        images.append(t / nu)
        combos.append([x / nu for x in b])
        hessen.append(c + [nu])

    def vdot(a, b):
        total = a[0] * b[0]
        for i in range(1, min(len(a), len(b))):
            total = total + a[i] * b[i]
        return total

    basis, upper = [], [[None] * ITERS for _ in range(ITERS)]
    for col in range(ITERS):
        column = list(hessen[col])
        for row in range(col):
            factor = vdot(basis[row], column)
            upper[row][col] = factor
            for i in range(len(basis[row])):
                column[i] = column[i] - factor * basis[row][i]
        norm = jnp.sqrt(vdot(column, column))
        upper[col][col] = norm
        basis.append([x / norm for x in column])
    y = [None] * ITERS
    for row in reversed(range(ITERS)):
        acc = basis[row][0] * beta
        for col in range(row + 1, ITERS):
            acc = acc - upper[row][col] * y[col]
        y[row] = acc / upper[row][row]
    e = []
    for i in range(ITERS + 1):
        acc = beta if i == 0 else jnp.zeros_like(beta)
        for col in range(ITERS):
            if i <= col + 1:
                acc = acc - hessen[col][i] * y[col]
        e.append(acc)
    sol, res = [], []
    for i in range(ITERS):
        acc = y[i] * combos[i][i]
        for j in range(i + 1, ITERS):
            acc = acc + y[j] * combos[j][i]
        sol.append(acc)
    for i in range(ITERS + 1):
        acc = e[i] * combos[i][i]
        for j in range(i + 1, ITERS + 1):
            acc = acc + e[j] * combos[j][i]
        res.append(acc)
    return sol, res


def kernel(sizes, r_ref, k_ref, s_ref, sol_ref, res_ref,
           sk, ksq, dinv, basis, last, za, zb, pk,
           ysend, yrecv, zsend, zrecv, crecv, red0, red1, red2, got1, got2,
           local_sem, gsend, grecv, xsend, xrecv, rsend1, rrecv1, rsend2, rrecv2):
    nx, ny, nz = sizes
    bx, by, bz = r_ref.shape
    rows = sk.shape[0]
    X, Y, Z = nx * bx, by + 2 * DEPTH, bz + LANES
    half = X // 2
    per = LANES // DEPTH
    groups = zsend.shape[-1] // LANES
    gx, gy, gz = lax.axis_index("gx"), lax.axis_index("gy"), lax.axis_index("gz")

    def wrap(i, n):
        return lax.rem(i + n, n)

    py, qy = wrap(gy - 1, ny), wrap(gy + 1, ny)
    pz, qz = wrap(gz - 1, nz), wrap(gz + 1, nz)

    plane_peers = []
    for dx in range(nx):
        for dy in range(ny):
            if dx or dy:
                plane_peers.append((wrap(gx + dx, nx), wrap(gy + dy, ny), gz))
    z_peers = [(gx, gy, wrap(gz + d, nz)) for d in range(1, nz)]
    diagonals = [(gx, py, pz), (gx, qy, pz), (gx, py, qz), (gx, qy, qz)]

    own_s = pltpu.make_async_copy(s_ref, sk, local_sem.at[0])
    own_k = pltpu.make_async_copy(
        k_ref, ksq.at[pl.ds(0, bx), pl.ds(0, by), pl.ds(0, bz)], local_sem.at[1])
    own_r = pltpu.make_async_copy(
        r_ref, basis.at[0, pl.ds(0, bx), pl.ds(0, by), pl.ds(0, bz)], local_sem.at[2])
    own_k.start()
    own_r.start()
    own_s.start()

    barrier = pltpu.get_barrier_semaphore()
    everyone = plane_peers + z_peers + diagonals
    for peer in everyone:
        pl.semaphore_signal(barrier, inc=1, device_id=peer, device_id_type=MESH)
    pl.semaphore_wait(barrier, len(everyone))

    gathers = []
    for which, src in ((0, k_ref), (1, r_ref)):
        for i in range(1, nx):
            dst = ksq if which == 0 else basis.at[0]
            copy = pltpu.make_async_remote_copy(
                src_ref=src,
                dst_ref=dst.at[pl.ds(i * bx, bx), pl.ds(0, by), pl.ds(0, bz)],
                send_sem=gsend.at[which, i - 1], recv_sem=grecv.at[which, i - 1],
                device_id=(wrap(gx - i, nx), gy, gz), device_id_type=MESH)
            copy.start()
            gathers.append((which, copy))

    sub_low = lax.broadcasted_iota(jnp.int32, (8, bz), 0) < DEPTH
    sub_low_z = lax.broadcasted_iota(jnp.int32, (8, zsend.shape[-1]), 0) < DEPTH
    lane_by = lax.broadcasted_iota(jnp.int32, (by, LANES), 1)
    lane_y = lax.broadcasted_iota(jnp.int32, (Y, LANES), 1)

    pending = []

    def exchange_start(slot, buf):
        def pack_y(p, carry):
            low0, low1 = buf[p, 0:8, 0:bz], buf[p + half, 0:8, 0:bz]
            high0, high1 = buf[p, by - 8:by, 0:bz], buf[p + half, by - 8:by, 0:bz]
            ysend[slot, 0, p] = jnp.where(sub_low, low0, pltpu.roll(low1, DEPTH, 0))
            ysend[slot, 1, p] = jnp.where(sub_low, pltpu.roll(high0, DEPTH, 0), high1)
            return carry

        planes(half, 4, pack_y, 0)
        copies = []

        def send(m, src, dst, peer):
            copy = pltpu.make_async_remote_copy(
                src_ref=src, dst_ref=dst, send_sem=xsend.at[slot, m], recv_sem=xrecv.at[slot, m],
                device_id=peer, device_id_type=MESH)
            copy.start()
            copies.append(copy)

        send(0, ysend.at[slot, 0], yrecv.at[slot, 0], (gx, py, gz))
        send(1, ysend.at[slot, 1], yrecv.at[slot, 1], (gx, qy, gz))
        for g in range(groups):
            def pack_z(p, carry):
                left, right = carry
                plane = g * per + p
                mine = lax.div(lane_by, DEPTH) == p
                first = pltpu.roll(buf[plane, 0:by, 0:LANES], DEPTH * p, 1)
                final = pltpu.roll(
                    buf[plane, 0:by, bz - LANES:bz], lax.rem(DEPTH * (p + 1), LANES), 1)
                return jnp.where(mine, first, left), jnp.where(mine, final, right)

            zero = jnp.zeros((by, LANES), jnp.float32)
            left, right = planes(min(per, X - g * per), 8, pack_z, (zero, zero))
            zsend[slot, 0, :, g * LANES:(g + 1) * LANES] = left
            zsend[slot, 1, :, g * LANES:(g + 1) * LANES] = right
        send(2, zsend.at[slot, 0], zrecv.at[slot, 0], (gx, gy, pz))
        send(3, zsend.at[slot, 1], zrecv.at[slot, 1], (gx, gy, qz))
        for m, (side, row, peer) in enumerate((
                (0, 0, (gx, py, pz)), (0, by - 8, (gx, qy, pz)),
                (1, 0, (gx, py, qz)), (1, by - 8, (gx, qy, qz)))):
            send(4 + m, zsend.at[slot, side, pl.ds(row, 8)], crecv.at[slot, m], peer)
        pending.extend(copies)
        return copies

    def exchange_finish(slot, buf, copies):
        copies[0].wait_recv()
        copies[1].wait_recv()

        def unpack_y(p, carry):
            up, down = yrecv[slot, 0, p], yrecv[slot, 1, p]
            buf[p, by:Y, 0:bz] = jnp.where(sub_low, up, pltpu.roll(down, DEPTH, 0))
            buf[p + half, by:Y, 0:bz] = jnp.where(sub_low, pltpu.roll(up, DEPTH, 0), down)
            return carry

        planes(half, 4, unpack_y, 0)
        for copy in copies[2:]:
            copy.wait_recv()
        right = jnp.concatenate(
            [zrecv[slot, 0], jnp.where(sub_low_z, crecv[slot, 0], crecv[slot, 1])], axis=0)
        left = jnp.concatenate(
            [zrecv[slot, 1], jnp.where(sub_low_z, crecv[slot, 2], crecv[slot, 3])], axis=0)
        for g in range(groups):
            right_g = right[:, g * LANES:(g + 1) * LANES]
            left_g = left[:, g * LANES:(g + 1) * LANES]

            def unpack_z(p, carry):
                high = pltpu.roll(right_g, lax.rem(LANES - DEPTH * p, LANES), 1)
                low = pltpu.roll(left_g, LANES - DEPTH - DEPTH * p, 1)
                tile = jnp.where(
                    lane_y < DEPTH, high, jnp.where(lane_y >= LANES - DEPTH, low, 0.0))
                buf[g * per + p, :, bz:Z] = tile
                return carry

            planes(min(per, X - g * per), 8, unpack_z, 0)

    def near(z_ref, p):
        centre = z_ref[p]
        total = z_ref[lax.rem(p + X - 1, X)] + z_ref[lax.rem(p + 1, X)]
        total = total + pltpu.roll(centre, 1, 0) + pltpu.roll(centre, Y - 1, 0)
        total = total + pltpu.roll(centre, 1, 1) + pltpu.roll(centre, Z - 1, 1)
        return centre, total

    def sketch(slot, plane_of):
        def body(p, acc):
            v = plane_of(p)
            out = []
            for row in range(rows):
                prod = sk[row, p] * v
                part = prod[:, 0:LANES]
                for i in range(1, bz // LANES):
                    part = part + prod[:, i * LANES:(i + 1) * LANES]
                tile = part[0:8]
                for i in range(1, by // 8):
                    tile = tile + part[8 * i:8 * i + 8]
                out.append(acc[row] + tile)
            return tuple(out)

        acc = planes(bx, 2, body, tuple(jnp.zeros((8, LANES), jnp.float32) for _ in range(rows)))
        for row in range(rows):
            red0[slot, pl.ds(row, 1)] = jnp.sum(acc[row], axis=0, keepdims=True)

    own_k.wait()
    for which, copy in gathers:
        if which == 0:
            copy.wait_recv()
    k_copies = exchange_start(0, ksq)
    own_r.wait()
    own_s.wait()
    sketch(0, lambda p: basis[0, p, 0:by, 0:bz])
    for which, copy in gathers:
        if which == 1:
            copy.wait_recv()
    copies = exchange_start(1, basis.at[0])
    exchange_finish(0, ksq, k_copies)

    def invert(p, carry):
        dinv[p] = 1.0 / (6.0 + ksq[p])
        return carry

    planes(X, 4, invert, 0)
    for it in range(ITERS):
        vec = basis.at[it]
        if it:
            sketch(it, lambda p: vec[p, 0:by, 0:bz])
        exchange_finish(it + 1, vec, copies)

        def scale(p, carry):
            za[p] = vec[p] * dinv[p]
            return carry

        planes(X, 4, scale, 0)
        src, dst = za, zb
        for sweep in range(SWEEPS):
            reach = SWEEPS - sweep
            shrunk = it == ITERS - 1 and bx + 2 * reach < X
            begin, count = (X - reach, bx + 2 * reach) if shrunk else (0, X)

            step = max(n for n in range(1, 9) if count % n == 0)

            def jacobi(at, carry):
                where = [lax.rem(begin + step * at + i, X) for i in range(step)]
                for p in where:
                    centre, total = near(src, p)
                    dst[p] = (vec[p] + total) * dinv[p]
                return carry

            lax.fori_loop(0, count // step, jacobi, 0)
            src, dst = dst, src

        def operate(at, carry):
            values = []
            for i in range(4):
                p = 4 * at + i
                centre, total = near(src, p)
                inner = centre[0:by, 0:bz]
                value = (6.0 - ksq[p, 0:by, 0:bz]) * inner - total[0:by, 0:bz]
                values.append(value - SHIFTS[it] * vec[p, 0:by, 0:bz])
            for i, value in enumerate(values):
                if it == ITERS - 1:
                    last[4 * at + i] = value
                else:
                    basis[it + 1, 4 * at + i, 0:by, 0:bz] = value
            return carry

        lax.fori_loop(0, (bx if it == ITERS - 1 else X) // 4, operate, 0)
        if it < ITERS - 1:
            copies = exchange_start(it + 2, basis.at[it + 1])

        def keep(p, carry):
            pk[it, p] = src[p, 0:by, 0:bz]
            return carry

        planes(bx, 4, keep, 0)
    sketch(ITERS, lambda p: last[p])

    lane_r = lax.broadcasted_iota(jnp.int32, (8, LANES), 1)
    table = jnp.zeros((8, LANES), jnp.float32)
    parts = rows // 8
    for j in range(ITERS + 1):
        for h in range(parts):
            table = jnp.where(
                lane_r == j * parts + h,
                jnp.sum(red0[j, pl.ds(8 * h, 8)], axis=1, keepdims=True), table)
    red1[...] = table
    for buf, got, peers, ssem, rsem, out in (
            (red1, got1, plane_peers, rsend1, rrecv1, red2), (red2, got2, z_peers, rsend2, rrecv2, None)):
        sums = []
        for m, peer in enumerate(peers):
            copy = pltpu.make_async_remote_copy(
                src_ref=buf, dst_ref=got.at[m], send_sem=ssem.at[m], recv_sem=rsem.at[m],
                device_id=peer, device_id_type=MESH)
            copy.start()
            sums.append(copy)
        total = buf[...]
        for m, copy in enumerate(sums):
            copy.wait_recv()
            total = total + got[m]
        pending.extend(sums)
        if out is not None:
            out[...] = total
    sketches = []
    for j in range(ITERS + 1):
        sketches.append(jnp.concatenate([
            jnp.broadcast_to(jnp.sum(
                jnp.where(lane_r == j * parts + h, total, 0.0), axis=1, keepdims=True), (8, LANES))
            for h in range(parts)], axis=0))
    sol, res = small_solve(sketches)
    wide = bz // LANES
    sol = [jnp.concatenate([c] * wide, axis=1) for c in sol]
    res = [jnp.concatenate([c] * wide, axis=1) for c in res]

    def combine(p, carry):
        acc = pk[0, p] * sol[0]
        for i in range(1, ITERS):
            acc = acc + pk[i, p] * sol[i]
        sol_ref[p] = acc
        acc = last[p] * res[ITERS]
        for i in range(ITERS):
            acc = acc + basis[i, p, 0:by, 0:bz] * res[i]
        res_ref[p] = acc
        return carry

    planes(bx, 2, combine, 0)
    for which, copy in gathers:
        copy.wait_send()
    for copy in pending:
        copy.wait_send()


def write_out(a_ref, b_ref, sol_ref, res_ref):
    sol_ref[...] = a_ref[...]
    res_ref[...] = b_ref[...]


def solution(mesh):
    nx, ny, nz = mesh.shape["gx"], mesh.shape["gy"], mesh.shape["gz"]

    def local(right_side, wavenumber_sq, sketch_matrix):
        rows, bx, by, bz = sketch_matrix.shape
        X, Y, Z = nx * bx, by + 2 * DEPTH, bz + LANES
        packed = -(-X * DEPTH // LANES) * LANES
        slots = ITERS + 1
        f32 = jnp.float32
        dma = pltpu.SemaphoreType.DMA
        plane, line = nx * ny - 1, nz - 1
        found = pl.pallas_call(
            functools.partial(kernel, (nx, ny, nz)),
            out_shape=(jax.ShapeDtypeStruct((bx, by, bz), f32),) * 2,
            in_specs=[pl.BlockSpec(memory_space=pl.ANY)] * 3,
            out_specs=[pl.BlockSpec(memory_space=pltpu.VMEM)] * 2,
            scratch_shapes=[
                pltpu.VMEM((rows, bx, by, bz), f32),
                pltpu.VMEM((X, Y, Z), f32),
                pltpu.VMEM((X, Y, Z), f32),
                pltpu.VMEM((ITERS, X, Y, Z), f32),
                pltpu.VMEM((bx, by, bz), f32),
                pltpu.VMEM((X, Y, Z), f32),
                pltpu.VMEM((X, Y, Z), f32),
                pltpu.VMEM((ITERS, bx, by, bz), f32),
                pltpu.VMEM((slots, 2, X // 2, 8, bz), f32),
                pltpu.VMEM((slots, 2, X // 2, 8, bz), f32),
                pltpu.VMEM((slots, 2, by, packed), f32),
                pltpu.VMEM((slots, 2, by, packed), f32),
                pltpu.VMEM((slots, 4, 8, packed), f32),
                pltpu.VMEM((slots, rows, LANES), f32),
                pltpu.VMEM((8, LANES), f32),
                pltpu.VMEM((8, LANES), f32),
                pltpu.VMEM((plane, 8, LANES), f32),
                pltpu.VMEM((line, 8, LANES), f32),
                dma((3,)),
                dma((2, nx - 1)), dma((2, nx - 1)),
                dma((slots, 8)), dma((slots, 8)),
                dma((plane,)), dma((plane,)),
                dma((line,)), dma((line,)),
            ],
            compiler_params=pltpu.CompilerParams(
                collective_id=0, has_side_effects=True, vmem_limit_bytes=60 * 1024 * 1024),
        )(right_side, wavenumber_sq, sketch_matrix)
        return pl.pallas_call(
            write_out,
            out_shape=(jax.ShapeDtypeStruct((bx, by, bz), f32),) * 2,
            in_specs=[pl.BlockSpec(memory_space=pltpu.VMEM)] * 2,
            out_specs=[pl.BlockSpec(memory_space=pltpu.VMEM)] * 2,
        )(*found)

    spec = P("gx", "gy", "gz")
    return jax.shard_map(
        local, mesh=mesh, in_specs=(spec, spec, P(None, "gx", "gy", "gz")),
        out_specs=(spec, spec), check_vma=False)
```

```python
import functools

import jax
import jax.numpy as jnp
from jax import lax
from jax.experimental import pallas as pl
from jax.experimental.pallas import tpu as pltpu
from jax.sharding import PartitionSpec as P

SWEEPS = 3
ITERS = 3
DEPTH = SWEEPS + 1
SHIFTS = (0.75, 0.5, 0.25)
MESH = pl.DeviceIdType.MESH
LANES = 128


def planes(count, step, body, carry):
    while count % step:
        step //= 2

    def group(at, carry):
        for i in range(step):
            carry = body(at * step + i, carry)
        return carry

    return lax.fori_loop(0, count // step, group, carry)


def small_solve(sketches):
    def dot(a, b):
        return jnp.sum(a * b, axis=0, keepdims=True)

    beta = jnp.sqrt(dot(sketches[0], sketches[0]))
    combos = [[1.0 / beta]]
    images = [sketches[0] / beta]
    hessen = []
    for it in range(ITERS):
        a = combos[it]
        b = [SHIFTS[i] * a[i] for i in range(it + 1)] + [None]
        for i in range(1, it + 2):
            b[i] = a[i - 1] if b[i] is None else b[i] + a[i - 1]
        s = b[0] * sketches[0]
        for i in range(1, it + 2):
            s = s + b[i] * sketches[i]
        c = [dot(images[i], s) for i in range(it + 1)]
        t = s
        for i in range(it + 1):
            t = t - c[i] * images[i]
            for m in range(i + 1):
                b[m] = b[m] - c[i] * combos[i][m]
        nu = jnp.sqrt(dot(t, t))
        images.append(t / nu)
        combos.append([x / nu for x in b])
        hessen.append(c + [nu])

    def vdot(a, b):
        total = a[0] * b[0]
        for i in range(1, min(len(a), len(b))):
            total = total + a[i] * b[i]
        return total

    basis, upper = [], [[None] * ITERS for _ in range(ITERS)]
    for col in range(ITERS):
        column = list(hessen[col])
        for row in range(col):
            factor = vdot(basis[row], column)
            upper[row][col] = factor
            for i in range(len(basis[row])):
                column[i] = column[i] - factor * basis[row][i]
        norm = jnp.sqrt(vdot(column, column))
        upper[col][col] = norm
        basis.append([x / norm for x in column])
    y = [None] * ITERS
    for row in reversed(range(ITERS)):
        acc = basis[row][0] * beta
        for col in range(row + 1, ITERS):
            acc = acc - upper[row][col] * y[col]
        y[row] = acc / upper[row][row]
    e = []
    for i in range(ITERS + 1):
        acc = beta if i == 0 else jnp.zeros_like(beta)
        for col in range(ITERS):
            if i <= col + 1:
                acc = acc - hessen[col][i] * y[col]
        e.append(acc)
    sol, res = [], []
    for i in range(ITERS):
        acc = y[i] * combos[i][i]
        for j in range(i + 1, ITERS):
            acc = acc + y[j] * combos[j][i]
        sol.append(acc)
    for i in range(ITERS + 1):
        acc = e[i] * combos[i][i]
        for j in range(i + 1, ITERS + 1):
            acc = acc + e[j] * combos[j][i]
        res.append(acc)
    return sol, res


def kernel(sizes, r_ref, k_ref, s_ref, sol_ref, res_ref,
           sk, ksq, dinv, base0, base1, base2, last, za, zb, pk,
           ysend, yrecv, zsend, zrecv, crecv, red0, red1, red2, got1, got2,
           local_sem, gsend, grecv, xsend, xrecv, rsend1, rrecv1, rsend2, rrecv2):
    basis = (base0, base1, base2)
    nx, ny, nz = sizes
    bx, by, bz = r_ref.shape
    rows = sk.shape[0]
    X, Y, Z = nx * bx, by + 2 * DEPTH, bz + LANES
    half = X // 2
    per = LANES // DEPTH
    groups = zsend.shape[-1] // LANES
    gx, gy, gz = lax.axis_index("gx"), lax.axis_index("gy"), lax.axis_index("gz")

    def wrap(i, n):
        return lax.rem(i + n, n)

    py, qy = wrap(gy - 1, ny), wrap(gy + 1, ny)
    pz, qz = wrap(gz - 1, nz), wrap(gz + 1, nz)

    plane_peers = []
    for dx in range(nx):
        for dy in range(ny):
            if dx or dy:
                plane_peers.append((wrap(gx + dx, nx), wrap(gy + dy, ny), gz))
    z_peers = [(gx, gy, wrap(gz + d, nz)) for d in range(1, nz)]
    diagonals = [(gx, py, pz), (gx, qy, pz), (gx, py, qz), (gx, qy, qz)]

    own_s = pltpu.make_async_copy(s_ref, sk, local_sem.at[0])
    own_k = pltpu.make_async_copy(
        k_ref, ksq.at[pl.ds(0, bx), pl.ds(0, by), pl.ds(0, bz)], local_sem.at[1])
    own_r = pltpu.make_async_copy(
        r_ref, basis[0].at[pl.ds(0, bx), pl.ds(0, by), pl.ds(0, bz)], local_sem.at[2])
    own_k.start()
    own_r.start()
    own_s.start()

    barrier = pltpu.get_barrier_semaphore()
    everyone = plane_peers + z_peers + diagonals
    for peer in everyone:
        pl.semaphore_signal(barrier, inc=1, device_id=peer, device_id_type=MESH)
    pl.semaphore_wait(barrier, len(everyone))

    gathers = []
    for which, src in ((0, k_ref), (1, r_ref)):
        for i in range(1, nx):
            dst = ksq if which == 0 else basis[0]
            copy = pltpu.make_async_remote_copy(
                src_ref=src,
                dst_ref=dst.at[pl.ds(i * bx, bx), pl.ds(0, by), pl.ds(0, bz)],
                send_sem=gsend.at[which, i - 1], recv_sem=grecv.at[which, i - 1],
                device_id=(wrap(gx - i, nx), gy, gz), device_id_type=MESH)
            copy.start()
            gathers.append((which, copy))

    sub_low = lax.broadcasted_iota(jnp.int32, (8, bz), 0) < DEPTH
    sub_low_z = lax.broadcasted_iota(jnp.int32, (8, zsend.shape[-1]), 0) < DEPTH
    lane_by = lax.broadcasted_iota(jnp.int32, (by, LANES), 1)
    lane_y = lax.broadcasted_iota(jnp.int32, (Y, LANES), 1)

    pending = []

    def exchange_start(slot, buf):
        def pack_y(p, carry):
            low0, low1 = buf[p, 0:8, 0:bz], buf[p + half, 0:8, 0:bz]
            high0, high1 = buf[p, by - 8:by, 0:bz], buf[p + half, by - 8:by, 0:bz]
            ysend[slot, 0, p] = jnp.where(sub_low, low0, pltpu.roll(low1, DEPTH, 0))
            ysend[slot, 1, p] = jnp.where(sub_low, pltpu.roll(high0, DEPTH, 0), high1)
            return carry

        planes(half, 4, pack_y, 0)
        copies = []

        def send(m, src, dst, peer):
            copy = pltpu.make_async_remote_copy(
                src_ref=src, dst_ref=dst, send_sem=xsend.at[slot, m], recv_sem=xrecv.at[slot, m],
                device_id=peer, device_id_type=MESH)
            copy.start()
            copies.append(copy)

        send(0, ysend.at[slot, 0], yrecv.at[slot, 0], (gx, py, gz))
        send(1, ysend.at[slot, 1], yrecv.at[slot, 1], (gx, qy, gz))
        for g in range(groups):
            def pack_z(p, carry):
                left, right = carry
                plane = g * per + p
                mine = lax.div(lane_by, DEPTH) == p
                first = pltpu.roll(buf[plane, 0:by, 0:LANES], DEPTH * p, 1)
                final = pltpu.roll(
                    buf[plane, 0:by, bz - LANES:bz], lax.rem(DEPTH * (p + 1), LANES), 1)
                return jnp.where(mine, first, left), jnp.where(mine, final, right)

            zero = jnp.zeros((by, LANES), jnp.float32)
            left, right = planes(min(per, X - g * per), 8, pack_z, (zero, zero))
            zsend[slot, 0, :, g * LANES:(g + 1) * LANES] = left
            zsend[slot, 1, :, g * LANES:(g + 1) * LANES] = right
        send(2, zsend.at[slot, 0], zrecv.at[slot, 0], (gx, gy, pz))
        send(3, zsend.at[slot, 1], zrecv.at[slot, 1], (gx, gy, qz))
        for m, (side, row, peer) in enumerate((
                (0, 0, (gx, py, pz)), (0, by - 8, (gx, qy, pz)),
                (1, 0, (gx, py, qz)), (1, by - 8, (gx, qy, qz)))):
            send(4 + m, zsend.at[slot, side, pl.ds(row, 8)], crecv.at[slot, m], peer)
        pending.extend(copies)
        return copies

    def exchange_finish(slot, buf, copies):
        copies[0].wait_recv()
        copies[1].wait_recv()

        def unpack_y(p, carry):
            up, down = yrecv[slot, 0, p], yrecv[slot, 1, p]
            buf[p, by:Y, 0:bz] = jnp.where(sub_low, up, pltpu.roll(down, DEPTH, 0))
            buf[p + half, by:Y, 0:bz] = jnp.where(sub_low, pltpu.roll(up, DEPTH, 0), down)
            return carry

        planes(half, 4, unpack_y, 0)
        for copy in copies[2:]:
            copy.wait_recv()
        right = jnp.concatenate(
            [zrecv[slot, 0], jnp.where(sub_low_z, crecv[slot, 0], crecv[slot, 1])], axis=0)
        left = jnp.concatenate(
            [zrecv[slot, 1], jnp.where(sub_low_z, crecv[slot, 2], crecv[slot, 3])], axis=0)
        for g in range(groups):
            right_g = right[:, g * LANES:(g + 1) * LANES]
            left_g = left[:, g * LANES:(g + 1) * LANES]

            def unpack_z(p, carry):
                high = pltpu.roll(right_g, lax.rem(LANES - DEPTH * p, LANES), 1)
                low = pltpu.roll(left_g, LANES - DEPTH - DEPTH * p, 1)
                tile = jnp.where(
                    lane_y < DEPTH, high, jnp.where(lane_y >= LANES - DEPTH, low, 0.0))
                buf[g * per + p, :, bz:Z] = tile
                return carry

            planes(min(per, X - g * per), 8, unpack_z, 0)

    def near(z_ref, p):
        centre = z_ref[p]
        total = z_ref[lax.rem(p + X - 1, X)] + z_ref[lax.rem(p + 1, X)]
        total = total + pltpu.roll(centre, 1, 0) + pltpu.roll(centre, Y - 1, 0)
        total = total + pltpu.roll(centre, 1, 1) + pltpu.roll(centre, Z - 1, 1)
        return centre, total

    def sketch(slot, plane_of):
        def body(p, acc):
            v = plane_of(p)
            out = []
            for row in range(rows):
                prod = sk[row, p] * v
                part = prod[:, 0:LANES]
                for i in range(1, bz // LANES):
                    part = part + prod[:, i * LANES:(i + 1) * LANES]
                tile = part[0:8]
                for i in range(1, by // 8):
                    tile = tile + part[8 * i:8 * i + 8]
                out.append(acc[row] + tile)
            return tuple(out)

        acc = planes(bx, 2, body, tuple(jnp.zeros((8, LANES), jnp.float32) for _ in range(rows)))
        for row in range(rows):
            red0[slot, pl.ds(row, 1)] = jnp.sum(acc[row], axis=0, keepdims=True)

    own_k.wait()
    for which, copy in gathers:
        if which == 0:
            copy.wait_recv()
    k_copies = exchange_start(0, ksq)
    own_r.wait()
    own_s.wait()
    sketch(0, lambda p: basis[0][p, 0:by, 0:bz])
    for which, copy in gathers:
        if which == 1:
            copy.wait_recv()
    copies = exchange_start(1, basis[0])
    exchange_finish(0, ksq, k_copies)

    def invert(p, carry):
        dinv[p] = 1.0 / (6.0 + ksq[p])
        return carry

    planes(X, 4, invert, 0)
    for it in range(ITERS):
        vec = basis[it]
        if it:
            sketch(it, lambda p: vec[p, 0:by, 0:bz])
        exchange_finish(it + 1, vec, copies)

        def scale(p, carry):
            za[p] = vec[p] * dinv[p]
            return carry

        planes(X, 4, scale, 0)
        src, dst = za, zb
        for sweep in range(SWEEPS):
            reach = SWEEPS - sweep
            shrunk = it == ITERS - 1 and bx + 2 * reach < X
            begin, count = (X - reach, bx + 2 * reach) if shrunk else (0, X)

            step = max(n for n in range(1, 9) if count % n == 0)

            def jacobi(at, carry):
                where = [lax.rem(begin + step * at + i, X) for i in range(step)]
                for p in where:
                    centre, total = near(src, p)
                    dst[p] = (vec[p] + total) * dinv[p]
                return carry

            lax.fori_loop(0, count // step, jacobi, 0)
            src, dst = dst, src

        def operate(p, carry):
            centre, total = near(src, p)
            inner = centre[0:by, 0:bz]
            value = (6.0 - ksq[p, 0:by, 0:bz]) * inner - total[0:by, 0:bz]
            value = value - SHIFTS[it] * vec[p, 0:by, 0:bz]
            if it == ITERS - 1:
                last[p] = value
            else:
                basis[it + 1][p, 0:by, 0:bz] = value
            return carry

        planes(bx if it == ITERS - 1 else X, 8, operate, 0)
        if it < ITERS - 1:
            copies = exchange_start(it + 2, basis[it + 1])

        def keep(p, carry):
            pk[it, p] = src[p, 0:by, 0:bz]
            return carry

        planes(bx, 4, keep, 0)
    sketch(ITERS, lambda p: last[p])

    lane_r = lax.broadcasted_iota(jnp.int32, (8, LANES), 1)
    table = jnp.zeros((8, LANES), jnp.float32)
    parts = rows // 8
    for j in range(ITERS + 1):
        for h in range(parts):
            table = jnp.where(
                lane_r == j * parts + h,
                jnp.sum(red0[j, pl.ds(8 * h, 8)], axis=1, keepdims=True), table)
    red1[...] = table
    for buf, got, peers, ssem, rsem, out in (
            (red1, got1, plane_peers, rsend1, rrecv1, red2), (red2, got2, z_peers, rsend2, rrecv2, None)):
        sums = []
        for m, peer in enumerate(peers):
            copy = pltpu.make_async_remote_copy(
                src_ref=buf, dst_ref=got.at[m], send_sem=ssem.at[m], recv_sem=rsem.at[m],
                device_id=peer, device_id_type=MESH)
            copy.start()
            sums.append(copy)
        total = buf[...]
        for m, copy in enumerate(sums):
            copy.wait_recv()
            total = total + got[m]
        pending.extend(sums)
        if out is not None:
            out[...] = total
    sketches = []
    for j in range(ITERS + 1):
        sketches.append(jnp.concatenate([
            jnp.broadcast_to(jnp.sum(
                jnp.where(lane_r == j * parts + h, total, 0.0), axis=1, keepdims=True), (8, LANES))
            for h in range(parts)], axis=0))
    sol, res = small_solve(sketches)
    wide = bz // LANES
    sol = [jnp.concatenate([c] * wide, axis=1) for c in sol]
    res = [jnp.concatenate([c] * wide, axis=1) for c in res]

    def combine(p, carry):
        acc = pk[0, p] * sol[0]
        for i in range(1, ITERS):
            acc = acc + pk[i, p] * sol[i]
        sol_ref[p] = acc
        acc = last[p] * res[ITERS]
        for i in range(ITERS):
            acc = acc + basis[i][p, 0:by, 0:bz] * res[i]
        res_ref[p] = acc
        return carry

    planes(bx, 2, combine, 0)
    for which, copy in gathers:
        copy.wait_send()
    for copy in pending:
        copy.wait_send()


def write_out(a_ref, b_ref, sol_ref, res_ref):
    sol_ref[...] = a_ref[...]
    res_ref[...] = b_ref[...]


def solution(mesh):
    nx, ny, nz = mesh.shape["gx"], mesh.shape["gy"], mesh.shape["gz"]

    def local(right_side, wavenumber_sq, sketch_matrix):
        rows, bx, by, bz = sketch_matrix.shape
        X, Y, Z = nx * bx, by + 2 * DEPTH, bz + LANES
        packed = -(-X * DEPTH // LANES) * LANES
        slots = ITERS + 1
        f32 = jnp.float32
        dma = pltpu.SemaphoreType.DMA
        plane, line = nx * ny - 1, nz - 1
        found = pl.pallas_call(
            functools.partial(kernel, (nx, ny, nz)),
            out_shape=(jax.ShapeDtypeStruct((bx, by, bz), f32),) * 2,
            in_specs=[pl.BlockSpec(memory_space=pl.ANY)] * 3,
            out_specs=[pl.BlockSpec(memory_space=pltpu.VMEM)] * 2,
            scratch_shapes=[
                pltpu.VMEM((rows, bx, by, bz), f32),
                pltpu.VMEM((X, Y, Z), f32),
                pltpu.VMEM((X, Y, Z), f32),
                pltpu.VMEM((X, Y, Z), f32),
                pltpu.VMEM((X, Y, Z), f32),
                pltpu.VMEM((X, Y, Z), f32),
                pltpu.VMEM((bx, by, bz), f32),
                pltpu.VMEM((X, Y, Z), f32),
                pltpu.VMEM((X, Y, Z), f32),
                pltpu.VMEM((ITERS, bx, by, bz), f32),
                pltpu.VMEM((slots, 2, X // 2, 8, bz), f32),
                pltpu.VMEM((slots, 2, X // 2, 8, bz), f32),
                pltpu.VMEM((slots, 2, by, packed), f32),
                pltpu.VMEM((slots, 2, by, packed), f32),
                pltpu.VMEM((slots, 4, 8, packed), f32),
                pltpu.VMEM((slots, rows, LANES), f32),
                pltpu.VMEM((8, LANES), f32),
                pltpu.VMEM((8, LANES), f32),
                pltpu.VMEM((plane, 8, LANES), f32),
                pltpu.VMEM((line, 8, LANES), f32),
                dma((3,)),
                dma((2, nx - 1)), dma((2, nx - 1)),
                dma((slots, 8)), dma((slots, 8)),
                dma((plane,)), dma((plane,)),
                dma((line,)), dma((line,)),
            ],
            compiler_params=pltpu.CompilerParams(
                collective_id=0, has_side_effects=True, vmem_limit_bytes=60 * 1024 * 1024),
        )(right_side, wavenumber_sq, sketch_matrix)
        return pl.pallas_call(
            write_out,
            out_shape=(jax.ShapeDtypeStruct((bx, by, bz), f32),) * 2,
            in_specs=[pl.BlockSpec(memory_space=pltpu.VMEM)] * 2,
            out_specs=[pl.BlockSpec(memory_space=pltpu.VMEM)] * 2,
        )(*found)

    spec = P("gx", "gy", "gz")
    return jax.shard_map(
        local, mesh=mesh, in_specs=(spec, spec, P(None, "gx", "gy", "gz")),
        out_specs=(spec, spec), check_vma=False)
```
